32 devices in a mesh: member: 8 (over y, x, core), space: 4 (over z).
Axes of the slice: x: 2, y: 2, z: 4, core: 2. Of those that a mesh axis runs over, the one named last changes fastest.
Arguments:
- background: bfloat16 [256, 4, 16384], P('member', None, 'space'), may hold values from -6 to 6
- obs_ens: float32 [256, 32768], P('member', 'space'), may hold values from -6 to 6
- observed: float32 [32768], P('space'), may hold values from -8 to 8
- variance: float32 [32768], P('space'), may hold values from 0.5 to 4
- obs_slot: int32 [4, 16, 512], P('space', 'member'), may hold values from 0 to 24575
- obs_count: int32 [4, 16], P('space', 'member'), may hold values from 256 to 512
- loc_bin: int32 [4, 16, 512], P('space', 'member'), may hold values from 0 to 31
Outputs:
- analysis: bfloat16 [256, 4, 16384], P('member', None, 'space')
The draws below stay inside these ranges and needn't reach their ends.
All inputs are finite; a program needn't handle non-finite values.
Results may differ from the reference program's by a relative error of at most 0.0056.
Values may be sent and summed in bfloat16 or wider, within the bound.
A program may use at most 192 MiB of HBM per device.

```python
import math
import jax
import jax.numpy as jnp
from jax import lax

K = 256
L = 4
OBS_LOC = 512
OBS_TILE = 8192
ITERS = 8
NBINS = 32
NTILE = 4
BLK_TILE = 16
NCOL = 16384
NOBS = 32768


def draw_obs_slot(key, part):
    top_value = 3 * OBS_TILE
    entries = NTILE * BLK_TILE * OBS_LOC
    key_vals, key_spot = jax.random.split(key, 2)
    values = jax.random.randint(key_vals, (entries,), 0, top_value, dtype=jnp.int32)
    spot_one = jax.random.randint(key_spot, (), 0, entries, dtype=jnp.int32)
    spot_two = (spot_one + 1) % entries
    values = values.at[spot_one].set(top_value - 1)
    values = values.at[spot_two].set(0)
    return values.reshape(NTILE, BLK_TILE, OBS_LOC)


def draw_obs_count(key, part):
    entries = NTILE * BLK_TILE
    key_vals, key_spot = jax.random.split(jax.random.fold_in(key, 7), 2)
    values = jax.random.randint(key_vals, (entries,), OBS_LOC // 2, OBS_LOC + 1, dtype=jnp.int32)
    spot_one = jax.random.randint(key_spot, (), 0, entries, dtype=jnp.int32)
    spot_two = (spot_one + 1) % entries
    values = values.at[spot_one].set(OBS_LOC)
    values = values.at[spot_two].set(OBS_LOC // 2)
    return values.reshape(NTILE, BLK_TILE)


def with_ends(array, key, low, largest):
    extent = array.shape
    index_at = [jax.random.randint(jax.random.fold_in(key, axis), (), 0, extent[axis]) for axis in range(len(extent))]
    array = array.at[tuple(index_at)].set(low)
    longest = extent.index(max(extent))
    index_at[longest] = (index_at[longest] + 1) % extent[longest]
    return array.at[tuple(index_at)].set(largest)


def shard_levels(rng, shape, cuts, low, high):
    level, own = 1.0, jax.random.fold_in(rng, 6)
    for position, shards_of in cuts:
        heights = jnp.exp(jax.random.uniform(jax.random.fold_in(own, position), (shards_of,), jnp.float32, low / len(cuts), high / len(cuts)))
        level = level * jnp.repeat(heights, shape[position] // shards_of).reshape([-1 if axis == position else 1 for axis in range(len(shape))])
    return level


def normal_values(stream_key, extent, scale, limit, cuts=(), kind=jnp.bfloat16):
    values = scale * jax.random.normal(stream_key, extent, jnp.float32)
    if cuts:
        values = values * shard_levels(stream_key, extent, cuts, -0.22, 0.18)
    return jnp.clip(values, -limit, limit).astype(kind)


def setup_inputs(seed: int = 0) -> dict:
    splits = jax.random.split(jax.random.key(seed), 8)
    background = normal_values(splits[0], (K, L, NCOL), 1.0, 6.0, ((0, 8), (2, 4)))
    obs_ens = normal_values(splits[1], (K, NOBS), 1.0, 6.0, ((0, 8), (1, 4)), jnp.float32)
    observed = normal_values(splits[2], (NOBS,), 2.0, 8.0, ((0, 4),), jnp.float32)
    variance = jnp.clip(jnp.exp(math.log(4.0) - 2.0794415 * jax.random.uniform(splits[3], (NOBS,), jnp.float32) ** shard_levels(splits[3], (NOBS,), ((0, 4),), -0.2, 0.2)), 0.5, 4.0)
    obs_slot = draw_obs_slot(jax.random.fold_in(splits[7], 71), 0)
    obs_count = draw_obs_count(jax.random.fold_in(splits[7], 71), 0)
    loc_bin = with_ends(jax.random.randint(splits[6], (NTILE, BLK_TILE, OBS_LOC), 0, NBINS), jax.random.fold_in(splits[6], 1), 0, NBINS - 1).astype(jnp.int32)
    return {"background": background, "obs_ens": obs_ens, "observed": observed, "variance": variance, "obs_slot": obs_slot, "obs_count": obs_count, "loc_bin": loc_bin}


def localize(bin_idx):
    scaled = bin_idx.astype(jnp.float32) / (NBINS * 0.375)
    return jnp.exp(-0.5 * scaled * scaled)

def transforms(columns, departure, weight):
    members = columns.shape[0]
    highest = lax.Precision.HIGHEST
    scaled = columns * weight[None]
    gram_mat = jnp.einsum('kbp,jbp->bkj', scaled, columns, precision=highest)
    identity = jnp.eye(members, dtype=jnp.float32)
    system = gram_mat + (members - 1.0) * identity[None]
    half_trace = 0.5 * jnp.trace(system, axis1=1, axis2=2)
    root_iter = system / half_trace[:, None, None]
    inv_root = jnp.broadcast_to(identity[None], root_iter.shape)
    for sweep_num in range(ITERS):
        correct = 1.5 * identity[None] - 0.5 * jnp.einsum('bij,bjk->bik', inv_root, root_iter, precision=highest)
        root_iter = jnp.einsum('bij,bjk->bik', root_iter, correct, precision=highest)
        inv_root = jnp.einsum('bij,bjk->bik', correct, inv_root, precision=highest)
    covariance = jnp.einsum('bij,bjk->bik', inv_root, inv_root, precision=highest) / half_trace[:, None, None]
    pulled = jnp.einsum('kbp,bp->bk', scaled, departure, precision=highest)
    mean_shift = jnp.einsum('bij,bj->bi', covariance, pulled, precision=highest)
    spread = inv_root * jnp.sqrt((members - 1.0) / half_trace)[:, None, None]
    return (spread + mean_shift[:, :, None]).astype(jnp.bfloat16)

def analyse(columns, weights_tot):
    members, levels, span_cols = columns.shape
    blocks = weights_tot.shape[0]
    average = lax.optimization_barrier(jnp.mean(columns.astype(jnp.float32), axis=0))
    perturb = (columns.astype(jnp.float32) - average[None]).astype(jnp.bfloat16)
    blocked = perturb.reshape(members, levels, blocks, span_cols // blocks)
    increment = jnp.einsum('klbc,bkn->nlbc', blocked.astype(jnp.float32), weights_tot.astype(jnp.float32), precision=lax.Precision.HIGHEST)
    return (increment.reshape(members, levels, span_cols) + average[None]).astype(jnp.bfloat16)

def reference(background, obs_ens, observed, variance, obs_slot, obs_count, loc_bin):
    tile_count = obs_slot.shape[0]
    members, levels, col_total = background.shape
    tile_obs = observed.shape[0] // tile_count
    tile_cols = col_total // tile_count
    obs_mean = lax.optimization_barrier(jnp.mean(obs_ens, axis=0))
    obs_pert = obs_ens - obs_mean[None]
    departure = observed - obs_mean
    field_view = background.reshape(members, levels, tile_count, tile_cols)

    def one_tile(tile_num):
        slot_idx = lax.dynamic_index_in_dim(obs_slot, tile_num, 0, keepdims=False)
        counts = lax.dynamic_index_in_dim(obs_count, tile_num, 0, keepdims=False)
        bin_idx = lax.dynamic_index_in_dim(loc_bin, tile_num, 0, keepdims=False)
        source = (tile_num - 1 + slot_idx // tile_obs) % tile_count
        global_idx = (source * tile_obs + slot_idx % tile_obs).astype(jnp.int32)
        columns = jnp.take(obs_pert, global_idx, axis=1)
        in_range = jnp.arange(slot_idx.shape[1], dtype=jnp.int32)[None, :] < counts[:, None]
        weight = jnp.where(in_range, localize(bin_idx) / variance[global_idx], 0.0)
        weights_tot = transforms(columns, departure[global_idx], weight)
        fields = lax.dynamic_index_in_dim(field_view, tile_num, 2, keepdims=False)
        return analyse(fields, weights_tot)
    result = lax.map(one_tile, jnp.arange(tile_count, dtype=jnp.int32))
    return jnp.moveaxis(result, 0, 2).reshape(members, levels, col_total)
```

```python
import jax
import jax.numpy as jnp
from jax import lax
from jax.experimental import pallas as pl
from jax.experimental.pallas import tpu as pltpu
from jax.sharding import PartitionSpec as P

ITERS = 8
NBINS = 32
F32 = jnp.float32
BF16 = jnp.bfloat16


def pick_kernel(slot_ref, before_ref, own_ref, after_ref, sbefore_ref, sown_ref, safter_ref,
                out_ref, side_ref, table, rows):
    members, tile_obs = own_ref.shape
    blocks, _, slots = out_ref.shape
    for k, (src, side) in enumerate(((before_ref, sbefore_ref), (own_ref, sown_ref), (after_ref, safter_ref))):
        @pl.loop(0, tile_obs // 512)
        def _(c, k=k, src=src, side=side):
            for u in range(4):
                at = pl.multiple_of(c * 512 + u * 128, 128)
                x = jnp.concatenate(
                    [src[:, pl.ds(at, 128)].astype(F32), side[:, pl.ds(at, 128)],
                     jnp.zeros((128 - members - 8, 128), F32)], axis=0)
                table[pl.ds(pl.multiple_of(k * tile_obs + at, 128), 128), :] = x.T

    @pl.loop(0, blocks)
    def _(b):
        @pl.loop(0, slots // 32)
        def _(g):
            base = pl.multiple_of(g * 32, 32)
            for u in range(32):
                i = slot_ref[b * slots + base + u]
                rows[pl.ds(base + u, 1), :] = table[pl.ds(i, 1), :]
        for u in range(slots // 128):
            t = rows[u * 128:(u + 1) * 128, :].T
            out_ref[b, :, u * 128:(u + 1) * 128] = t[:members].astype(BF16)
            side_ref[b, :, u * 128:(u + 1) * 128] = t[members:members + 8]


def pick(slots, tables, sides, blocks, width):
    members, tile_obs = tables[0].shape
    vmem = pl.BlockSpec(memory_space=pltpu.VMEM)
    return pl.pallas_call(
        pick_kernel,
        out_shape=(jax.ShapeDtypeStruct((blocks, members, width), BF16),
                   jax.ShapeDtypeStruct((blocks, 8, width), F32)),
        in_specs=[pl.BlockSpec(memory_space=pltpu.SMEM)] + [vmem] * 6,
        out_specs=(vmem, vmem),
        scratch_shapes=[pltpu.VMEM((3 * tile_obs, 128), F32), pltpu.VMEM((width, 128), F32)],
        compiler_params=pltpu.CompilerParams(vmem_limit_bytes=50 * 2**20),
        name="pick",
    )(slots, *tables, *sides)


def dot1(a, b, nt=False):
    dims = (((1,), (1 if nt else 0,)), ((), ()))
    return lax.dot_general(a.astype(BF16), b.astype(BF16), dims, preferred_element_type=F32)


def dot3(a, b):
    ah, bh = a.astype(BF16), b.astype(BF16)
    al, bl = (a - ah.astype(F32)).astype(BF16), (b - bh.astype(F32)).astype(BF16)
    return dot1(ah, bh) + (dot1(ah, bl) + dot1(al, bh))


def eye(n):
    return (lax.broadcasted_iota(jnp.int32, (n, n), 0) == lax.broadcasted_iota(jnp.int32, (n, n), 1)).astype(F32)


def roots(x, observed, variance, loc_bin, count):
    members, slots = x[0].shape
    ident = eye(members)
    ys, zs, halves, pulls = [], [], [], []
    for b in range(len(x)):
        mean = jnp.sum(x[b], axis=0, keepdims=True) * (1.0 / members)
        pert = x[b] - mean
        scaled = loc_bin[b].astype(F32) / (NBINS * 0.375)
        weight = jnp.exp(-0.5 * scaled * scaled) / variance[b]
        weight = jnp.where(lax.broadcasted_iota(jnp.int32, (1, slots), 1) < count[b], weight, 0.0)
        root_w = pert * jnp.sqrt(weight)
        gram = dot1(root_w, root_w, nt=True)
        system = gram + (members - 1.0) * ident
        half = 0.5 * jnp.sum(system * ident)
        pulls.append(jnp.sum(pert * (weight * (observed[b] - mean)), axis=1, keepdims=True))
        halves.append(half)
        ys.append(system / half)
        zs.append(None)
    for sweep in range(ITERS):
        for b in range(len(x)):
            y, z = ys[b], zs[b]
            if z is None:
                m = y
                zs[b] = 1.5 * ident - 0.5 * m
                ys[b] = 1.5 * y - 0.5 * dot1(y, m)
                continue
            m = dot1(z, y) if sweep < ITERS - 2 else dot3(z, y)
            if sweep < ITERS - 3:
                zs[b] = 1.5 * z - 0.5 * dot1(m, z)
                ys[b] = 1.5 * y - 0.5 * dot1(y, m)
            else:
                e = ident - m
                zs[b] = z + 0.5 * dot1(e, z)
                if sweep < ITERS - 1:
                    ys[b] = y + 0.5 * dot1(y, e)
    return zs, halves, pulls


def weights_t(z, half, pulled):
    members = z.shape[0]
    ident = eye(members)
    inner = jnp.sum(z * pulled, axis=0, keepdims=True)
    shift = jnp.sum(z * inner, axis=1, keepdims=True) / half
    shift_row = jnp.sum(shift * ident, axis=0, keepdims=True)
    return (jnp.sqrt((members - 1.0) / half) * z + shift_row).astype(BF16)


def spread_levels(wt, levels):
    members = wt.shape[0]
    n = members * levels
    r0 = lax.broadcasted_iota(jnp.int32, (n, members), 0) // levels
    up = (r0 == lax.broadcasted_iota(jnp.int32, (n, members), 1)).astype(BF16)
    tall = dot1(up, wt)
    wide = dot1(tall, up, nt=True)
    same = (lax.broadcasted_iota(jnp.int32, (n, n), 0) % levels) == (lax.broadcasted_iota(jnp.int32, (n, n), 1) % levels)
    return jnp.where(same, wide, 0.0).astype(BF16)


def analyse(f, w4, levels):
    n, cols = f.shape
    members = n // levels
    f = f.astype(F32).reshape(n // 8, 8, cols)
    total = jnp.sum(f, axis=0)
    step = levels
    while step < 8:
        total = total + pltpu.roll(total, step, 0)
        step *= 2
    mean = total * (1.0 / members)
    pert = (f - mean[None]).reshape(n, cols)
    inc = dot1(w4, pert)
    return (inc.reshape(n // 8, 8, cols) + mean[None]).reshape(n, cols).astype(BF16)


def main_kernel(count_ref, levels, picks_ref, side_ref, bin_ref, field_ref, out_ref):
    parts, blocks, share, slots = picks_ref.shape
    members = parts * share
    rows, cols = field_ref.shape[0] * field_ref.shape[1], field_ref.shape[2]
    cut = cols // blocks
    x = [picks_ref[:, b].reshape(members, slots).astype(F32) for b in range(blocks)]
    zs, halves, pulls = roots(
        x, [side_ref[b, 0:1] for b in range(blocks)], [side_ref[b, 1:2] for b in range(blocks)],
        [bin_ref[b:b + 1] for b in range(blocks)], [count_ref[b] for b in range(blocks)])
    for b in range(blocks):
        w4 = spread_levels(weights_t(zs[b], halves[b], pulls[b]), levels)
        f = field_ref[:, :, b * cut:(b + 1) * cut].reshape(rows, cut)
        out_ref[:, :, b * cut:(b + 1) * cut] = analyse(f, w4, levels).reshape(parts, rows // parts, cut)


def per_device(background, obs_ens, observed, variance, obs_slot, obs_count, loc_bin):
    devices = lax.axis_size("member")
    space = lax.axis_size("space")
    share, levels, columns = background.shape
    blocks, width = obs_slot.shape[1:]
    up = [(i, (i + 1) % space) for i in range(space)]
    down = [(j, i) for i, j in up]
    own = obs_ens.astype(BF16)
    side = jnp.concatenate([observed[None], variance[None], jnp.zeros((6, observed.shape[0]), F32)], axis=0)
    tables = (lax.ppermute(own, "space", up), own, lax.ppermute(own, "space", down))
    short = side[:2]
    grow = lambda s: jnp.concatenate([s, jnp.zeros((6, s.shape[1]), F32)], axis=0)
    sides = (grow(lax.ppermute(short, "space", up)), side, grow(lax.ppermute(short, "space", down)))
    every_slot = lax.all_gather(obs_slot[0], "member", axis=0, tiled=True).reshape(-1)
    picked, picked_side = pick(every_slot, tables, sides, devices * blocks, width)
    picked = picked.reshape(devices, blocks, share, width)
    picks = lax.all_to_all(picked, "member", split_axis=0, concat_axis=0, tiled=True)
    mine = lax.dynamic_slice_in_dim(picked_side, lax.axis_index("member") * blocks, blocks, 0)
    flat = background.reshape(share * levels, devices, columns // devices).transpose(1, 0, 2)
    fields = lax.all_to_all(flat, "member", split_axis=0, concat_axis=0, tiled=True)
    vmem = pl.BlockSpec(memory_space=pltpu.VMEM)
    out = pl.pallas_call(
        lambda c, *refs: main_kernel(c, levels, *refs),
        out_shape=jax.ShapeDtypeStruct(fields.shape, BF16),
        in_specs=[pl.BlockSpec(memory_space=pltpu.SMEM)] + [vmem] * 4,
        out_specs=vmem,
        compiler_params=pltpu.CompilerParams(vmem_limit_bytes=50 * 2**20),
        name="analysis",
    )(obs_count[0], picks, mine, loc_bin[0], fields)
    back = lax.all_to_all(out, "member", split_axis=0, concat_axis=0, tiled=True)
    return back.transpose(1, 0, 2).reshape(share, levels, columns)


def solution(mesh):
    in_specs = (
        P("member", None, "space"), P("member", "space"), P("space"), P("space"),
        P("space", "member", None), P("space", "member"), P("space", "member", None),
    )
    return jax.shard_map(per_device, mesh=mesh, in_specs=in_specs,
                         out_specs=P("member", None, "space"), check_vma=False)
```

```python
import functools

import jax
import jax.numpy as jnp
from jax import lax
from jax.experimental import pallas as pl
from jax.experimental.pallas import tpu as pltpu
from jax.sharding import PartitionSpec as P

ITERS = 8
NBINS = 32
F32 = jnp.float32
BF16 = jnp.bfloat16


def pick_kernel(slot_ref, before_ref, own_ref, after_ref, sbefore_ref, sown_ref, safter_ref,
                out_ref, side_ref, table, rows):
    members, tile_obs = own_ref.shape
    blocks, _, slots = out_ref.shape
    for k, (src, side) in enumerate(((before_ref, sbefore_ref), (own_ref, sown_ref), (after_ref, safter_ref))):
        @pl.loop(0, tile_obs // 512)
        def _(c, k=k, src=src, side=side):
            for u in range(4):
                at = pl.multiple_of(c * 512 + u * 128, 128)
                line = c * 4 + u
                x = jnp.concatenate(
                    [src[:, pl.ds(at, 128)].astype(F32), side[pl.ds(line, 1), :],
                     side[pl.ds(line + tile_obs // 128, 1), :],
                     jnp.zeros((128 - members - 2, 128), F32)], axis=0)
                table[pl.ds(pl.multiple_of(k * tile_obs + at, 128), 128), :] = x.T

    @pl.loop(0, blocks)
    def _(b):
        @pl.loop(0, slots // 32)
        def _(g):
            base = pl.multiple_of(g * 32, 32)
            for u in range(32):
                i = slot_ref[b * slots + base + u]
                rows[pl.ds(base + u, 1), :] = table[pl.ds(i, 1), :]
        for u in range(slots // 128):
            t = rows[u * 128:(u + 1) * 128, :].T
            out_ref[b, :, u * 128:(u + 1) * 128] = t[:members].astype(BF16)
            side_ref[b, :, u * 128:(u + 1) * 128] = t[members:members + 8]


def pick(slots, tables, sides, blocks, width):
    members, tile_obs = tables[0].shape
    vmem = pl.BlockSpec(memory_space=pltpu.VMEM)
    return pl.pallas_call(
        pick_kernel,
        out_shape=(jax.ShapeDtypeStruct((blocks, members, width), BF16),
                   jax.ShapeDtypeStruct((blocks, 8, width), F32)),
        in_specs=[pl.BlockSpec(memory_space=pltpu.SMEM)] + [vmem] * 6,
        out_specs=(vmem, vmem),
        scratch_shapes=[pltpu.VMEM((3 * tile_obs, 128), F32), pltpu.VMEM((width, 128), F32)],
        compiler_params=pltpu.CompilerParams(vmem_limit_bytes=50 * 2**20),
        name="pick",
    )(slots, *tables, *sides)


def dot1(a, b, nt=False):
    dims = (((1,), (1 if nt else 0,)), ((), ()))
    return lax.dot_general(a.astype(BF16), b.astype(BF16), dims, preferred_element_type=F32)


def dot3(a, b):
    ah, bh = a.astype(BF16), b.astype(BF16)
    al, bl = (a - ah.astype(F32)).astype(BF16), (b - bh.astype(F32)).astype(BF16)
    return dot1(ah, bh) + (dot1(ah, bl) + dot1(al, bh))


def eye(n):
    return (lax.broadcasted_iota(jnp.int32, (n, n), 0) == lax.broadcasted_iota(jnp.int32, (n, n), 1)).astype(F32)


def roots(x, observed, variance, loc_bin, count):
    members, slots = x[0].shape
    ident = eye(members)
    ys, zs, halves, pulls = [], [], [], []
    for b in range(len(x)):
        mean = jnp.sum(x[b], axis=0, keepdims=True) * (1.0 / members)
        pert = x[b] - mean
        scaled = loc_bin[b].astype(F32) / (NBINS * 0.375)
        weight = jnp.exp(-0.5 * scaled * scaled) / variance[b]
        weight = jnp.where(lax.broadcasted_iota(jnp.int32, (1, slots), 1) < count[b], weight, 0.0)
        root_w = pert * jnp.sqrt(weight)
        gram = dot1(root_w, root_w, nt=True)
        system = gram + (members - 1.0) * ident
        half = 0.5 * jnp.sum(system * ident)
        pulls.append(jnp.sum(pert * (weight * (observed[b] - mean)), axis=1, keepdims=True))
        halves.append(half)
        ys.append(system / half)
        zs.append(None)
    for sweep in range(ITERS):
        for b in range(len(x)):
            y, z = ys[b], zs[b]
            if z is None:
                m = y
                zs[b] = 1.5 * ident - 0.5 * m
                ys[b] = 1.5 * y - 0.5 * dot1(y, m)
                continue
            m = dot1(z, y) if sweep < ITERS - 2 else dot3(z, y)
            if sweep < ITERS - 3:
                zs[b] = 1.5 * z - 0.5 * dot1(m, z)
                ys[b] = 1.5 * y - 0.5 * dot1(y, m)
            else:
                e = ident - m
                zs[b] = z + 0.5 * dot1(e, z)
                if sweep < ITERS - 1:
                    ys[b] = y + 0.5 * dot1(y, e)
    return zs, halves, pulls


def weights_t(z, half, pulled):
    members = z.shape[0]
    ident = eye(members)
    inner = jnp.sum(z * pulled, axis=0, keepdims=True)
    shift = jnp.sum(z * inner, axis=1, keepdims=True) / half
    shift_row = jnp.sum(shift * ident, axis=0, keepdims=True)
    return (jnp.sqrt((members - 1.0) / half) * z + shift_row).astype(BF16)


def spread_levels(wt, levels):
    members = wt.shape[0]
    n = members * levels
    r0 = lax.broadcasted_iota(jnp.int32, (n, members), 0) // levels
    up = (r0 == lax.broadcasted_iota(jnp.int32, (n, members), 1)).astype(BF16)
    tall = dot1(up, wt)
    wide = dot1(tall, up, nt=True)
    same = (lax.broadcasted_iota(jnp.int32, (n, n), 0) % levels) == (lax.broadcasted_iota(jnp.int32, (n, n), 1) % levels)
    return jnp.where(same, wide, 0.0).astype(BF16)


def analyse(f, w4, levels):
    n, cols = f.shape
    members = n // levels
    f = f.astype(F32).reshape(n // 8, 8, cols)
    total = jnp.sum(f, axis=0)
    step = levels
    while step < 8:
        total = total + pltpu.roll(total, step, 0)
        step *= 2
    mean = total * (1.0 / members)
    pert = (f - mean[None]).reshape(n, cols)
    inc = dot1(w4, pert)
    return (inc.reshape(n // 8, 8, cols) + mean[None]).reshape(n, cols).astype(BF16)


def greet(devices, me, space, here):
    barrier = pltpu.get_barrier_semaphore()
    for k in range(1, devices):
        pl.semaphore_signal(barrier, inc=1, device_id={"member": lax.rem(me + k, devices)},
                            device_id_type=pl.DeviceIdType.MESH)
    if space:
        for k in (1, space - 1):
            pl.semaphore_signal(barrier, inc=1, device_id={"space": lax.rem(here + k, space)},
                                device_id_type=pl.DeviceIdType.MESH)
    pl.semaphore_wait(barrier, devices - 1 + (2 if space else 0))


def send(src, dst, sems, at, axis, target):
    return pltpu.make_async_remote_copy(
        src_ref=src, dst_ref=dst, send_sem=sems[0].at[at], recv_sem=sems[1].at[at],
        device_id={axis: target}, device_id_type=pl.DeviceIdType.MESH)


def exchange_kernel(devices, space, own_ref, side_ref, slot_ref, field_ref,
                    before_ref, after_ref, sbefore_ref, safter_ref, slots_ref, fields_ref,
                    halo_send, halo_recv, slot_send, slot_recv, field_send, field_recv, local):
    me, here = lax.axis_index("member"), lax.axis_index("space")
    cols = field_ref.shape[1] // devices
    lines = slot_ref.shape[0]
    window = lambda d: pl.ds(pl.multiple_of(d * cols, 128), cols)
    mine = pl.ds(pl.multiple_of(me * lines, 8), lines)
    keep = [pltpu.make_async_copy(slot_ref, slots_ref.at[mine], local.at[0]),
            pltpu.make_async_copy(field_ref.at[:, window(me)], fields_ref.at[me], local.at[1])]
    greet(devices, me, space, here)
    halo = (halo_send, halo_recv)
    up, down = lax.rem(here + 1, space), lax.rem(here + space - 1, space)
    copies = [send(own_ref, before_ref, halo, 0, "space", up), send(own_ref, after_ref, halo, 1, "space", down),
              send(side_ref, sbefore_ref, halo, 2, "space", up), send(side_ref, safter_ref, halo, 3, "space", down)]
    for k in range(1, devices):
        to = lax.rem(me + k, devices)
        copies.append(send(slot_ref, slots_ref.at[mine], (slot_send, slot_recv), k, "member", to))
    for k in range(1, devices):
        to = lax.rem(me + k, devices)
        copies.append(send(field_ref.at[:, window(to)], fields_ref.at[me], (field_send, field_recv), k, "member", to))
    for copy in copies + keep:
        copy.start()
    for copy in copies + keep:
        copy.wait()


def main_kernel(levels, count_ref, picks_ref, side_ref, bin_ref, field_ref, out_ref,
                met, made, pick_send, pick_recv, out_send, out_recv):
    parts, blocks, share, slots = picks_ref.shape
    members = parts * share
    rows, cols = field_ref.shape[0] * field_ref.shape[1], field_ref.shape[2]
    cut = cols // blocks
    me = lax.axis_index("member")
    greet(parts, me, 0, 0)
    copies = []
    for k in range(1, parts):
        to = lax.rem(me + k, parts)
        copies.append(send(picks_ref.at[to], met.at[me], (pick_send, pick_recv), k, "member", to))
    for copy in copies:
        copy.start()
    met[me] = picks_ref[me]
    for copy in copies:
        copy.wait()
    x = [met[:, b].reshape(members, slots).astype(F32) for b in range(blocks)]
    zs, halves, pulls = roots(
        x, [side_ref[b, 0:1] for b in range(blocks)], [side_ref[b, 1:2] for b in range(blocks)],
        [bin_ref[b:b + 1] for b in range(blocks)], [count_ref[b] for b in range(blocks)])
    copies = []
    for b in range(blocks):
        w4 = spread_levels(weights_t(zs[b], halves[b], pulls[b]), levels)
        f = field_ref[:, :, b * cut:(b + 1) * cut].reshape(rows, cut)
        made[b] = analyse(f, w4, levels).reshape(parts, rows // parts, cut)
        window = pl.ds(pl.multiple_of(me * cols + b * cut, 128), cut)
        for k in range(1, parts):
            to = lax.rem(me + k, parts)
            copy = send(made.at[b, to], out_ref.at[:, window], (out_send.at[b], out_recv.at[b]), k, "member", to)
            copy.start()
            copies.append(copy)
        out_ref[:, window] = made[b, me]
    for copy in copies:
        copy.wait()


def per_device(background, obs_ens, observed, variance, obs_slot, obs_count, loc_bin):
    devices = lax.axis_size("member")
    space = lax.axis_size("space")
    share, levels, columns = background.shape
    blocks, width = obs_slot.shape[1:]
    rows, cols = share * levels, columns // devices
    own = obs_ens.astype(BF16)
    side = jnp.concatenate([observed.reshape(-1, 128), variance.reshape(-1, 128)], axis=0)
    slots = obs_slot.reshape(-1, 128)
    flat = background.reshape(rows, columns)
    hbm = pl.BlockSpec(memory_space=pl.ANY)
    vmem = pl.BlockSpec(memory_space=pltpu.VMEM)
    dma = lambda *n: pltpu.SemaphoreType.DMA(n)
    like = jax.ShapeDtypeStruct
    before, after, sbefore, safter, every_slot, fields = pl.pallas_call(
        functools.partial(exchange_kernel, devices, space),
        out_shape=(like(own.shape, BF16), like(own.shape, BF16), like(side.shape, F32), like(side.shape, F32),
                   like((devices * slots.shape[0], 128), jnp.int32), like((devices, rows, cols), BF16)),
        in_specs=[hbm] * 4,
        out_specs=(hbm,) * 6,
        scratch_shapes=[dma(4), dma(4), dma(devices), dma(devices), dma(devices), dma(devices), dma(2)],
        compiler_params=pltpu.CompilerParams(collective_id=0, has_side_effects=True),
        name="exchange",
    )(own, side, slots, flat)
    picked, picked_side = pick(every_slot.reshape(-1), (before, own, after), (sbefore, side, safter),
                               devices * blocks, width)
    picked = picked.reshape(devices, blocks, share, width)
    mine = lax.dynamic_slice_in_dim(picked_side, lax.axis_index("member") * blocks, blocks, 0)
    out = pl.pallas_call(
        functools.partial(main_kernel, levels),
        out_shape=like((rows, columns), BF16),
        in_specs=[pl.BlockSpec(memory_space=pltpu.SMEM)] + [vmem] * 4,
        out_specs=vmem,
        scratch_shapes=[pltpu.VMEM(picked.shape, BF16), pltpu.VMEM((blocks, devices, rows, cols // blocks), BF16),
                        dma(devices), dma(devices), dma(blocks, devices), dma(blocks, devices)],
        compiler_params=pltpu.CompilerParams(collective_id=1, has_side_effects=True, vmem_limit_bytes=50 * 2**20),
        name="analysis",
    )(obs_count[0], picked, mine, loc_bin[0], fields)
    return out.reshape(share, levels, columns)


def solution(mesh):
    in_specs = (
        P("member", None, "space"), P("member", "space"), P("space"), P("space"),
        P("space", "member", None), P("space", "member"), P("space", "member", None),
    )
    return jax.shard_map(per_device, mesh=mesh, in_specs=in_specs,
                         out_specs=P("member", None, "space"), check_vma=False)
```

```python
import functools

import jax
import jax.numpy as jnp
from jax import lax
from jax.experimental import pallas as pl
from jax.experimental.pallas import tpu as pltpu
from jax.sharding import PartitionSpec as P

ITERS = 8
NBINS = 32
F32 = jnp.float32
BF16 = jnp.bfloat16


def fill(table, src, side, base):
    members, tile_obs = src.shape

    @pl.loop(0, tile_obs // 512)
    def _(c):
        for u in range(4):
            at = pl.multiple_of(c * 512 + u * 128, 128)
            line = c * 4 + u
            x = jnp.concatenate(
                [src[:, pl.ds(at, 128)].astype(F32), side[pl.ds(line, 1), :],
                 side[pl.ds(line + tile_obs // 128, 1), :],
                 jnp.zeros((128 - members - 2, 128), F32)], axis=0)
            table[pl.ds(pl.multiple_of(base + at, 128), 128), :] = x.T


def dot1(a, b, nt=False):
    dims = (((1,), (1 if nt else 0,)), ((), ()))
    return lax.dot_general(a.astype(BF16), b.astype(BF16), dims, preferred_element_type=F32)


def dot3(a, b):
    ah, bh = a.astype(BF16), b.astype(BF16)
    al, bl = (a - ah.astype(F32)).astype(BF16), (b - bh.astype(F32)).astype(BF16)
    return dot1(ah, bh) + (dot1(ah, bl) + dot1(al, bh))


def eye(n):
    return (lax.broadcasted_iota(jnp.int32, (n, n), 0) == lax.broadcasted_iota(jnp.int32, (n, n), 1)).astype(F32)


def roots(x, observed, variance, loc_bin, count):
    members, slots = x[0].shape
    ident = eye(members)
    ys, zs, halves, pulls = [], [], [], []
    for b in range(len(x)):
        mean = jnp.sum(x[b], axis=0, keepdims=True) * (1.0 / members)
        pert = x[b] - mean
        scaled = loc_bin[b].astype(F32) / (NBINS * 0.375)
        weight = jnp.exp(-0.5 * scaled * scaled) / variance[b]
        weight = jnp.where(lax.broadcasted_iota(jnp.int32, (1, slots), 1) < count[b], weight, 0.0)
        root_w = pert * jnp.sqrt(weight)
        gram = dot1(root_w, root_w, nt=True)
        system = gram + (members - 1.0) * ident
        half = 0.5 * jnp.sum(system * ident)
        pulls.append(jnp.sum(pert * (weight * (observed[b] - mean)), axis=1, keepdims=True))
        halves.append(half)
        ys.append(system / half)
        zs.append(None)
    for sweep in range(ITERS):
        for b in range(len(x)):
            y, z = ys[b], zs[b]
            if z is None:
                m = y
                zs[b] = 1.5 * ident - 0.5 * m
                ys[b] = 1.5 * y - 0.5 * dot1(y, m)
                continue
            m = dot1(z, y) if sweep < ITERS - 2 else dot3(z, y)
            if sweep < ITERS - 3:
                zs[b] = 1.5 * z - 0.5 * dot1(m, z)
                ys[b] = 1.5 * y - 0.5 * dot1(y, m)
            else:
                e = ident - m
                zs[b] = z + 0.5 * dot1(e, z)
                if sweep < ITERS - 1:
                    ys[b] = y + 0.5 * dot1(y, e)
    return zs, halves, pulls


def weights_t(z, half, pulled):
    members = z.shape[0]
    ident = eye(members)
    inner = jnp.sum(z * pulled, axis=0, keepdims=True)
    shift = jnp.sum(z * inner, axis=1, keepdims=True) / half
    shift_row = jnp.sum(shift * ident, axis=0, keepdims=True)
    return (jnp.sqrt((members - 1.0) / half) * z + shift_row).astype(BF16)


def spread_levels(wt, levels):
    members = wt.shape[0]
    n = members * levels
    r0 = lax.broadcasted_iota(jnp.int32, (n, members), 0) // levels
    up = (r0 == lax.broadcasted_iota(jnp.int32, (n, members), 1)).astype(BF16)
    tall = dot1(up, wt)
    wide = dot1(tall, up, nt=True)
    same = (lax.broadcasted_iota(jnp.int32, (n, n), 0) % levels) == (lax.broadcasted_iota(jnp.int32, (n, n), 1) % levels)
    return jnp.where(same, wide, 0.0).astype(BF16)


def analyse(f, w4, levels):
    n, cols = f.shape
    members = n // levels
    f = f.astype(F32).reshape(n // 8, 8, cols)
    total = jnp.sum(f, axis=0)
    step = levels
    while step < 8:
        total = total + pltpu.roll(total, step, 0)
        step *= 2
    mean = total * (1.0 / members)
    pert = (f - mean[None]).reshape(n, cols)
    inc = dot1(w4, pert)
    return (inc.reshape(n // 8, 8, cols) + mean[None]).reshape(n, cols).astype(BF16)


def greet(devices, me, space, here):
    barrier = pltpu.get_barrier_semaphore()
    for k in range(1, devices):
        pl.semaphore_signal(barrier, inc=1, device_id={"member": lax.rem(me + k, devices)},
                            device_id_type=pl.DeviceIdType.MESH)
    if space:
        for k in (1, space - 1):
            pl.semaphore_signal(barrier, inc=1, device_id={"space": lax.rem(here + k, space)},
                                device_id_type=pl.DeviceIdType.MESH)
    pl.semaphore_wait(barrier, devices - 1 + (2 if space else 0))


def send(src, dst, sems, at, axis, target):
    return pltpu.make_async_remote_copy(
        src_ref=src, dst_ref=dst, send_sem=sems[0].at[at], recv_sem=sems[1].at[at],
        device_id={axis: target}, device_id_type=pl.DeviceIdType.MESH)


def main_kernel(devices, space, levels, count_ref, own_ref, side_ref, slot_ref, bin_ref, field_ref, out_ref,
                table, picked_rows, before, after, sbefore, safter, slots_met, slots_smem, fields,
                picks, met, side_met, made, local, halo_send, halo_recv, slot_send, slot_recv,
                field_send, field_recv, pick_send, pick_recv, out_send, out_recv):
    parts, blocks, share, slots = picks.shape
    members = parts * share
    tile_obs = own_ref.shape[1]
    rows, cols = fields.shape[0] * fields.shape[1], fields.shape[2]
    cut = cols // blocks
    me, here = lax.axis_index("member"), lax.axis_index("space")
    lines = slot_ref.shape[0]
    per = lines // blocks
    window = lambda d: pl.ds(pl.multiple_of(d * cols, 128), cols)
    mine = pl.ds(pl.multiple_of(me * lines, 8), lines)
    keep = pltpu.make_async_copy(field_ref.at[:, window(me)], fields.at[me], local.at[0])
    keep.start()
    greet(devices, me, space, here)
    halo = (halo_send, halo_recv)
    up, down = lax.rem(here + 1, space), lax.rem(here + space - 1, space)
    halo_copies = [send(own_ref, before, halo, 0, "space", up), send(own_ref, after, halo, 1, "space", down),
                   send(side_ref, sbefore, halo, 2, "space", up), send(side_ref, safter, halo, 3, "space", down)]
    for copy in halo_copies:
        copy.start()
    slot_copies, field_copies, pick_copies = [], [], []
    for k in range(1, devices):
        to = lax.rem(me + k, devices)
        slot_copies.append(send(slot_ref, slots_met.at[mine], (slot_send, slot_recv), k, "member", to))
        field_copies.append(send(field_ref.at[:, window(to)], fields.at[me], (field_send, field_recv), k, "member", to))
        pick_copies.append(send(picks.at[to], met.at[me], (pick_send, pick_recv), k, "member", to))
    for copy in slot_copies:
        copy.start()
    slots_met[mine, :] = slot_ref[...]
    fill(table, own_ref, side_ref, tile_obs)
    for copy in slot_copies:
        copy.wait()
    to_smem = pltpu.make_async_copy(slots_met, slots_smem, local.at[1])
    to_smem.start()
    to_smem.wait()
    for copy in halo_copies:
        copy.wait()
    for copy in field_copies:
        copy.start()
    fill(table, before, sbefore, 0)
    fill(table, after, safter, 2 * tile_obs)

    def pick_for(to, own):
        @pl.loop(0, lines)
        def _(r):
            for u in range(128):
                i = slots_smem[to * lines + r, u]
                picked_rows[u:u + 1, :] = table[pl.ds(i, 1), :]
            t = picked_rows[...].T
            block = r // per
            at = pl.ds(pl.multiple_of((r % per) * 128, 128), 128)
            if own:
                met[to, block, :, at] = t[:share].astype(BF16)
                side_met[block, :, at] = t[share:share + 8]
            else:
                picks[to, block, :, at] = t[:share].astype(BF16)

    @pl.loop(1, devices)
    def _(k):
        to = lax.rem(me + k, devices)
        pick_for(to, False)
        send(picks.at[to], met.at[me], (pick_send, pick_recv), k, "member", to).start()

    pick_for(me, True)
    for copy in pick_copies:
        copy.wait()
    x = [met[:, b].reshape(members, slots).astype(F32) for b in range(blocks)]
    zs, halves, pulls = roots(
        x, [side_met[b, 0:1] for b in range(blocks)], [side_met[b, 1:2] for b in range(blocks)],
        [bin_ref[b:b + 1] for b in range(blocks)], [count_ref[b] for b in range(blocks)])
    keep.wait()
    for copy in field_copies:
        copy.wait()
    copies = []
    for b in range(blocks):
        w4 = spread_levels(weights_t(zs[b], halves[b], pulls[b]), levels)
        f = fields[:, :, b * cut:(b + 1) * cut].reshape(rows, cut)
        made[b] = analyse(f, w4, levels).reshape(parts, rows // parts, cut)
        window = pl.ds(pl.multiple_of(me * cols + b * cut, 128), cut)
        for k in range(1, parts):
            to = lax.rem(me + k, parts)
            copy = send(made.at[b, to], out_ref.at[:, window], (out_send.at[b], out_recv.at[b]), k, "member", to)
            copy.start()
            copies.append(copy)
        out_ref[:, window] = made[b, me]
    for copy in copies:
        copy.wait()


def per_device(background, obs_ens, observed, variance, obs_slot, obs_count, loc_bin):
    devices = lax.axis_size("member")
    space = lax.axis_size("space")
    share, levels, columns = background.shape
    blocks, width = obs_slot.shape[1:]
    rows, cols = share * levels, columns // devices
    own = obs_ens.astype(BF16)
    side = jnp.concatenate([observed.reshape(-1, 128), variance.reshape(-1, 128)], axis=0)
    slots = obs_slot.reshape(-1, 128)
    flat = background.reshape(rows, columns)
    hbm = pl.BlockSpec(memory_space=pl.ANY)
    vmem = pl.BlockSpec(memory_space=pltpu.VMEM)
    dma = lambda *n: pltpu.SemaphoreType.DMA(n)
    like = jax.ShapeDtypeStruct
    out = pl.pallas_call(
        functools.partial(main_kernel, devices, space, levels),
        out_shape=like((rows, columns), BF16),
        in_specs=[pl.BlockSpec(memory_space=pltpu.SMEM)] + [vmem] * 4 + [hbm],
        out_specs=vmem,
        scratch_shapes=[
            pltpu.VMEM((3 * own.shape[1], 128), F32), pltpu.VMEM((128, 128), F32),
            pltpu.VMEM(own.shape, BF16), pltpu.VMEM(own.shape, BF16),
            pltpu.VMEM(side.shape, F32), pltpu.VMEM(side.shape, F32),
            pltpu.VMEM((devices * slots.shape[0], 128), jnp.int32), pltpu.SMEM((devices * slots.shape[0], 128), jnp.int32),
            pltpu.VMEM((devices, rows, cols), BF16),
            pltpu.VMEM((devices, blocks, share, width), BF16), pltpu.VMEM((devices, blocks, share, width), BF16),
            pltpu.VMEM((blocks, 8, width), F32), pltpu.VMEM((blocks, devices, rows, cols // blocks), BF16),
            dma(2), dma(4), dma(4)] + [dma(devices)] * 6 + [dma(blocks, devices)] * 2,
        compiler_params=pltpu.CompilerParams(collective_id=0, has_side_effects=True, vmem_limit_bytes=50 * 2**20),
        name="analysis",
    )(obs_count[0], own, side, slots, loc_bin[0], flat)
    return out.reshape(share, levels, columns)


def solution(mesh):
    in_specs = (
        P("member", None, "space"), P("member", "space"), P("space"), P("space"),
        P("space", "member", None), P("space", "member"), P("space", "member", None),
    )
    return jax.shard_map(per_device, mesh=mesh, in_specs=in_specs,
                         out_specs=P("member", None, "space"), check_vma=False)
```

```python
import functools

import jax
import jax.numpy as jnp
from jax import lax
from jax.experimental import pallas as pl
from jax.experimental.pallas import tpu as pltpu
from jax.sharding import PartitionSpec as P

ITERS = 8
NBINS = 32
CHUNKS = 4
F32 = jnp.float32
BF16 = jnp.bfloat16


def fill(table, src, side, base, first, width):
    members, tile_obs = src.shape

    @pl.loop(first // 512, (first + width) // 512)
    def _(c):
        for u in range(4):
            at = pl.multiple_of(c * 512 + u * 128, 128)
            line = c * 4 + u
            x = jnp.concatenate(
                [src[:, pl.ds(at, 128)].astype(F32), side[pl.ds(line, 1), :],
                 side[pl.ds(line + tile_obs // 128, 1), :],
                 jnp.zeros((128 - members - 2, 128), F32)], axis=0)
            table[pl.ds(pl.multiple_of(base + at, 128), 128), :] = x.T


def dot1(a, b, nt=False):
    dims = (((1,), (1 if nt else 0,)), ((), ()))
    return lax.dot_general(a.astype(BF16), b.astype(BF16), dims, preferred_element_type=F32)


def dot3(a, b):
    ah, bh = a.astype(BF16), b.astype(BF16)
    al, bl = (a - ah.astype(F32)).astype(BF16), (b - bh.astype(F32)).astype(BF16)
    return dot1(ah, bh) + (dot1(ah, bl) + dot1(al, bh))


def eye(n):
    return (lax.broadcasted_iota(jnp.int32, (n, n), 0) == lax.broadcasted_iota(jnp.int32, (n, n), 1)).astype(F32)


def roots(x, observed, variance, loc_bin, count):
    members, slots = x[0].shape
    ident = eye(members)
    ys, zs, halves, pulls = [], [], [], []
    for b in range(len(x)):
        mean = jnp.sum(x[b], axis=0, keepdims=True) * (1.0 / members)
        pert = x[b] - mean
        scaled = loc_bin[b].astype(F32) / (NBINS * 0.375)
        weight = jnp.exp(-0.5 * scaled * scaled) / variance[b]
        weight = jnp.where(lax.broadcasted_iota(jnp.int32, (1, slots), 1) < count[b], weight, 0.0)
        root_w = pert * jnp.sqrt(weight)
        gram = dot1(root_w, root_w, nt=True)
        system = gram + (members - 1.0) * ident
        half = 0.5 * jnp.sum(system * ident)
        pulls.append(jnp.sum(pert * (weight * (observed[b] - mean)), axis=1, keepdims=True))
        halves.append(half)
        ys.append(system / half)
        zs.append(None)
    for sweep in range(ITERS):
        for b in range(len(x)):
            y, z = ys[b], zs[b]
            if z is None:
                m = y
                zs[b] = 1.5 * ident - 0.5 * m
                ys[b] = 1.5 * y - 0.5 * dot1(y, m)
                continue
            m = dot1(z, y) if sweep < ITERS - 2 else dot3(z, y)
            if sweep < ITERS - 3:
                zs[b] = 1.5 * z - 0.5 * dot1(m, z)
                ys[b] = 1.5 * y - 0.5 * dot1(y, m)
            else:
                e = ident - m
                zs[b] = z + 0.5 * dot1(e, z)
                if sweep < ITERS - 1:
                    ys[b] = y + 0.5 * dot1(y, e)
    return zs, halves, pulls


def weights_t(z, half, pulled):
    members = z.shape[0]
    ident = eye(members)
    inner = jnp.sum(z * pulled, axis=0, keepdims=True)
    shift = jnp.sum(z * inner, axis=1, keepdims=True) / half
    shift_row = jnp.sum(shift * ident, axis=0, keepdims=True)
    return (jnp.sqrt((members - 1.0) / half) * z + shift_row).astype(BF16)


def spread_levels(wt, levels):
    members = wt.shape[0]
    n = members * levels
    r0 = lax.broadcasted_iota(jnp.int32, (n, members), 0) // levels
    up = (r0 == lax.broadcasted_iota(jnp.int32, (n, members), 1)).astype(BF16)
    tall = dot1(up, wt)
    wide = dot1(tall, up, nt=True)
    same = (lax.broadcasted_iota(jnp.int32, (n, n), 0) % levels) == (lax.broadcasted_iota(jnp.int32, (n, n), 1) % levels)
    return jnp.where(same, wide, 0.0).astype(BF16)


def analyse(f, w4, levels):
    n, cols = f.shape
    members = n // levels
    f = f.astype(F32).reshape(n // 8, 8, cols)
    total = jnp.sum(f, axis=0)
    step = levels
    while step < 8:
        total = total + pltpu.roll(total, step, 0)
        step *= 2
    mean = total * (1.0 / members)
    pert = (f - mean[None]).reshape(n, cols)
    inc = dot1(w4, pert)
    return (inc.reshape(n // 8, 8, cols) + mean[None]).reshape(n, cols).astype(BF16)


def greet(devices, me, space, here):
    barrier = pltpu.get_barrier_semaphore()
    for k in range(1, devices):
        pl.semaphore_signal(barrier, inc=1, device_id={"member": lax.rem(me + k, devices)},
                            device_id_type=pl.DeviceIdType.MESH)
    if space:
        for k in (1, space - 1):
            pl.semaphore_signal(barrier, inc=1, device_id={"space": lax.rem(here + k, space)},
                                device_id_type=pl.DeviceIdType.MESH)
    pl.semaphore_wait(barrier, devices - 1 + (2 if space else 0))


def send(src, dst, sems, at, axis, target):
    return pltpu.make_async_remote_copy(
        src_ref=src, dst_ref=dst, send_sem=sems[0].at[at], recv_sem=sems[1].at[at],
        device_id={axis: target}, device_id_type=pl.DeviceIdType.MESH)


def main_kernel(devices, space, levels, count_ref, own_ref, side_ref, slot_ref, bin_ref, field_ref, out_ref,
                table, picked_rows, before, after, sbefore, safter, slots_met, slots_smem, fields,
                picks, met, side_met, made, local, halo_send, halo_recv, slot_send, slot_recv,
                field_send, field_recv, pick_send, pick_recv, out_send, out_recv):
    parts, blocks, share, slots = picks.shape
    members = parts * share
    tile_obs = own_ref.shape[1]
    rows, cols = fields.shape[0] * fields.shape[1], fields.shape[2]
    cut = cols // blocks
    me, here = lax.axis_index("member"), lax.axis_index("space")
    lines = slot_ref.shape[0]
    per = lines // blocks
    window = lambda d: pl.ds(pl.multiple_of(d * cols, 128), cols)
    mine = pl.ds(pl.multiple_of(me * lines, 8), lines)
    keep = pltpu.make_async_copy(field_ref.at[:, window(me)], fields.at[me], local.at[0])
    keep.start()
    greet(devices, me, space, here)
    halo = (halo_send, halo_recv)
    up, down = lax.rem(here + 1, space), lax.rem(here + space - 1, space)
    side_copies = [send(side_ref, sbefore, halo, 0, "space", up), send(side_ref, safter, halo, 1, "space", down)]
    piece = tile_obs // CHUNKS
    halo_copies = []
    for c in range(CHUNKS):
        part = pl.ds(c * piece, piece)
        halo_copies.append(send(own_ref.at[:, part], before.at[:, part], halo, 2 + 2 * c, "space", up))
        halo_copies.append(send(own_ref.at[:, part], after.at[:, part], halo, 3 + 2 * c, "space", down))
    for copy in side_copies + halo_copies:
        copy.start()
    slot_copies, field_copies, pick_copies = [], [], []
    for k in range(1, devices):
        to = lax.rem(me + k, devices)
        slot_copies.append(send(slot_ref, slots_met.at[mine], (slot_send, slot_recv), k, "member", to))
        field_copies.append(send(field_ref.at[:, window(to)], fields.at[me], (field_send, field_recv), k, "member", to))
        pick_copies.append(send(picks.at[to], met.at[me], (pick_send, pick_recv), k, "member", to))
    for copy in slot_copies:
        copy.start()
    slots_met[mine, :] = slot_ref[...]
    fill(table, own_ref, side_ref, tile_obs, 0, tile_obs)
    for copy in slot_copies:
        copy.wait()
    to_smem = pltpu.make_async_copy(slots_met, slots_smem, local.at[1])
    to_smem.start()
    to_smem.wait()
    for copy in side_copies:
        copy.wait()
    for c in range(CHUNKS):
        halo_copies[2 * c].wait()
        fill(table, before, sbefore, 0, c * piece, piece)
        halo_copies[2 * c + 1].wait()
        if c == CHUNKS - 1:
            for copy in field_copies:
                copy.start()
        fill(table, after, safter, 2 * tile_obs, c * piece, piece)

    def pick_for(to, own):
        @pl.loop(0, lines)
        def _(r):
            for u in range(128):
                i = slots_smem[to * lines + r, u]
                picked_rows[u:u + 1, :] = table[pl.ds(i, 1), :]
            t = picked_rows[...].T
            block = r // per
            at = pl.ds(pl.multiple_of((r % per) * 128, 128), 128)
            if own:
                met[to, block, :, at] = t[:share].astype(BF16)
                side_met[block, :, at] = t[share:share + 8]
            else:
                picks[to, block, :, at] = t[:share].astype(BF16)

    @pl.loop(1, devices)
    def _(k):
        to = lax.rem(me + k, devices)
        pick_for(to, False)
        send(picks.at[to], met.at[me], (pick_send, pick_recv), k, "member", to).start()

    pick_for(me, True)
    for copy in pick_copies:
        copy.wait()
    copies = []
    for b in range(blocks):
        x = met[:, b].reshape(members, slots).astype(F32)
        zs, halves, pulls = roots(
            [x], [side_met[b, 0:1]], [side_met[b, 1:2]], [bin_ref[b:b + 1]], [count_ref[b]])
        w4 = spread_levels(weights_t(zs[0], halves[0], pulls[0]), levels)
        if b == 0:
            keep.wait()
            for copy in field_copies:
                copy.wait()
        f = fields[:, :, b * cut:(b + 1) * cut].reshape(rows, cut)
        made[b] = analyse(f, w4, levels).reshape(parts, rows // parts, cut)
        window = pl.ds(pl.multiple_of(me * cols + b * cut, 128), cut)
        for k in range(1, parts):
            to = lax.rem(me + k, parts)
            copy = send(made.at[b, to], out_ref.at[:, window], (out_send.at[b], out_recv.at[b]), k, "member", to)
            copy.start()
            copies.append(copy)
        out_ref[:, window] = made[b, me]
    for copy in copies:
        copy.wait()


def per_device(background, obs_ens, observed, variance, obs_slot, obs_count, loc_bin):
    devices = lax.axis_size("member")
    space = lax.axis_size("space")
    share, levels, columns = background.shape
    blocks, width = obs_slot.shape[1:]
    rows, cols = share * levels, columns // devices
    own = obs_ens.astype(BF16)
    side = jnp.concatenate([observed.reshape(-1, 128), variance.reshape(-1, 128)], axis=0)
    slots = obs_slot.reshape(-1, 128)
    flat = background.reshape(rows, columns)
    hbm = pl.BlockSpec(memory_space=pl.ANY)
    vmem = pl.BlockSpec(memory_space=pltpu.VMEM)
    dma = lambda *n: pltpu.SemaphoreType.DMA(n)
    like = jax.ShapeDtypeStruct
    out = pl.pallas_call(
        functools.partial(main_kernel, devices, space, levels),
        out_shape=like((rows, columns), BF16),
        in_specs=[pl.BlockSpec(memory_space=pltpu.SMEM)] + [vmem] * 4 + [hbm],
        out_specs=vmem,
        scratch_shapes=[
            pltpu.VMEM((3 * own.shape[1], 128), F32), pltpu.VMEM((128, 128), F32),
            pltpu.VMEM(own.shape, BF16), pltpu.VMEM(own.shape, BF16),
            pltpu.VMEM(side.shape, F32), pltpu.VMEM(side.shape, F32),
            pltpu.VMEM((devices * slots.shape[0], 128), jnp.int32), pltpu.SMEM((devices * slots.shape[0], 128), jnp.int32),
            pltpu.VMEM((devices, rows, cols), BF16),
            pltpu.VMEM((devices, blocks, share, width), BF16), pltpu.VMEM((devices, blocks, share, width), BF16),
            pltpu.VMEM((blocks, 8, width), F32), pltpu.VMEM((blocks, devices, rows, cols // blocks), BF16),
            dma(2), dma(2 + 2 * CHUNKS), dma(2 + 2 * CHUNKS)] + [dma(devices)] * 6 + [dma(blocks, devices)] * 2,
        compiler_params=pltpu.CompilerParams(collective_id=0, has_side_effects=True, vmem_limit_bytes=50 * 2**20),
        name="analysis",
    )(obs_count[0], own, side, slots, loc_bin[0], flat)
    return out.reshape(share, levels, columns)


def solution(mesh):
    in_specs = (
        P("member", None, "space"), P("member", "space"), P("space"), P("space"),
        P("space", "member", None), P("space", "member"), P("space", "member", None),
    )
    return jax.shard_map(per_device, mesh=mesh, in_specs=in_specs,
                         out_specs=P("member", None, "space"), check_vma=False)
```

```python
import functools

import jax
import jax.numpy as jnp
from jax import lax
from jax.experimental import pallas as pl
from jax.experimental.pallas import tpu as pltpu
from jax.sharding import PartitionSpec as P

ITERS = 8
NBINS = 32
CHUNKS = 4
F32 = jnp.float32
BF16 = jnp.bfloat16


def fill(table, src, side, base, first, width):
    members, tile_obs = src.shape

    @pl.loop(first // 512, (first + width) // 512)
    def _(c):
        for u in range(4):
            at = pl.multiple_of(c * 512 + u * 128, 128)
            line = c * 4 + u
            x = jnp.concatenate(
                [src[:, pl.ds(at, 128)].astype(F32), side[pl.ds(line, 1), :],
                 side[pl.ds(line + tile_obs // 128, 1), :],
                 jnp.zeros((128 - members - 2, 128), F32)], axis=0)
            table[pl.ds(pl.multiple_of(base + at, 128), 128), :] = x.T


def dot1(a, b, nt=False):
    dims = (((1,), (1 if nt else 0,)), ((), ()))
    return lax.dot_general(a.astype(BF16), b.astype(BF16), dims, preferred_element_type=F32)


def dot3(a, b):
    ah, bh = a.astype(BF16), b.astype(BF16)
    al, bl = (a - ah.astype(F32)).astype(BF16), (b - bh.astype(F32)).astype(BF16)
    return dot1(ah, bh) + (dot1(ah, bl) + dot1(al, bh))


def eye(n):
    return (lax.broadcasted_iota(jnp.int32, (n, n), 0) == lax.broadcasted_iota(jnp.int32, (n, n), 1)).astype(F32)


def roots(x, observed, variance, loc_bin, count):
    members, slots = x[0].shape
    ident = eye(members)
    ys, zs, halves, pulls = [], [], [], []
    for b in range(len(x)):
        mean = jnp.sum(x[b], axis=0, keepdims=True) * (1.0 / members)
        pert = x[b] - mean
        scaled = loc_bin[b].astype(F32) / (NBINS * 0.375)
        weight = jnp.exp(-0.5 * scaled * scaled) / variance[b]
        weight = jnp.where(lax.broadcasted_iota(jnp.int32, (1, slots), 1) < count[b], weight, 0.0)
        root_w = pert * jnp.sqrt(weight)
        gram = dot1(root_w, root_w, nt=True)
        system = gram + (members - 1.0) * ident
        half = 0.5 * jnp.sum(system * ident)
        pulls.append(jnp.sum(pert * (weight * (observed[b] - mean)), axis=1, keepdims=True))
        halves.append(half)
        ys.append(system / half)
        zs.append(None)
    for sweep in range(ITERS):
        for b in range(len(x)):
            y, z = ys[b], zs[b]
            if z is None:
                m = y
                zs[b] = 1.5 * ident - 0.5 * m
                ys[b] = 1.5 * y - 0.5 * dot1(y, m)
                continue
            m = dot1(z, y) if sweep < ITERS - 2 else dot3(z, y)
            if sweep < ITERS - 3:
                zs[b] = 1.5 * z - 0.5 * dot1(m, z)
                ys[b] = 1.5 * y - 0.5 * dot1(y, m)
            else:
                e = ident - m
                zs[b] = z + 0.5 * dot1(e, z)
                if sweep < ITERS - 1:
                    ys[b] = y + 0.5 * dot1(y, e)
    return zs, halves, pulls


def weights_t(z, half, pulled):
    members = z.shape[0]
    ident = eye(members)
    inner = jnp.sum(z * pulled, axis=0, keepdims=True)
    shift = jnp.sum(z * inner, axis=1, keepdims=True) / half
    shift_row = jnp.sum(shift * ident, axis=0, keepdims=True)
    return (jnp.sqrt((members - 1.0) / half) * z + shift_row).astype(BF16)


def spread_levels(wt, levels):
    members = wt.shape[0]
    n = members * levels
    r0 = lax.broadcasted_iota(jnp.int32, (n, members), 0) // levels
    up = (r0 == lax.broadcasted_iota(jnp.int32, (n, members), 1)).astype(BF16)
    tall = dot1(up, wt)
    wide = dot1(tall, up, nt=True)
    same = (lax.broadcasted_iota(jnp.int32, (n, n), 0) % levels) == (lax.broadcasted_iota(jnp.int32, (n, n), 1) % levels)
    return jnp.where(same, wide, 0.0).astype(BF16)


def analyse(f, w4, levels):
    n, cols = f.shape
    members = n // levels
    f = f.astype(F32).reshape(n // 8, 8, cols)
    total = jnp.sum(f, axis=0)
    step = levels
    while step < 8:
        total = total + pltpu.roll(total, step, 0)
        step *= 2
    mean = total * (1.0 / members)
    pert = (f - mean[None]).reshape(n, cols)
    inc = dot1(w4, pert)
    return (inc.reshape(n // 8, 8, cols) + mean[None]).reshape(n, cols).astype(BF16)


def greet(devices, me, space, here):
    barrier = pltpu.get_barrier_semaphore()
    for k in range(1, devices):
        pl.semaphore_signal(barrier, inc=1, device_id={"member": lax.rem(me + k, devices)},
                            device_id_type=pl.DeviceIdType.MESH)
    if space:
        for k in (1, space - 1):
            pl.semaphore_signal(barrier, inc=1, device_id={"space": lax.rem(here + k, space)},
                                device_id_type=pl.DeviceIdType.MESH)
    pl.semaphore_wait(barrier, devices - 1 + (2 if space else 0))


def send(src, dst, sems, at, axis, target):
    return pltpu.make_async_remote_copy(
        src_ref=src, dst_ref=dst, send_sem=sems[0].at[at], recv_sem=sems[1].at[at],
        device_id={axis: target}, device_id_type=pl.DeviceIdType.MESH)


def main_kernel(devices, space, levels, count_ref, own_ref, side_ref, slot_ref, bin_ref, field_ref, out_ref,
                table, picked_rows, before, after, sbefore, safter, slots_met, slots_smem, fields,
                picks, met, side_met, made, local, halo_send, halo_recv, slot_send, slot_recv,
                field_send, field_recv, pick_send, pick_recv, out_send, out_recv):
    parts, blocks, share, slots = picks.shape
    members = parts * share
    tile_obs = own_ref.shape[1]
    rows, cols = fields.shape[0] * fields.shape[1], fields.shape[2]
    cut = cols // blocks
    me, here = lax.axis_index("member"), lax.axis_index("space")
    lines = slot_ref.shape[0]
    per = lines // blocks
    window = lambda d: pl.ds(pl.multiple_of(d * cols, 128), cols)
    mine = pl.ds(pl.multiple_of(me * lines, 8), lines)
    keep = pltpu.make_async_copy(field_ref.at[:, window(me)], fields.at[me], local.at[0])
    keep.start()
    greet(devices, me, space, here)
    halo = (halo_send, halo_recv)
    up, down = lax.rem(here + 1, space), lax.rem(here + space - 1, space)
    side_copies = [send(side_ref, sbefore, halo, 0, "space", up), send(side_ref, safter, halo, 1, "space", down)]
    piece = tile_obs // CHUNKS
    halo_copies = []
    for c in range(CHUNKS):
        part = pl.ds(c * piece, piece)
        halo_copies.append(send(own_ref.at[:, part], before.at[:, part], halo, 2 + 2 * c, "space", up))
        halo_copies.append(send(own_ref.at[:, part], after.at[:, part], halo, 3 + 2 * c, "space", down))
    for copy in side_copies + halo_copies:
        copy.start()
    slot_copies, field_copies, pick_copies = [], [], []
    for k in range(1, devices):
        to = lax.rem(me + k, devices)
        slot_copies.append(send(slot_ref, slots_met.at[mine], (slot_send, slot_recv), k, "member", to))
        field_copies.append(send(field_ref.at[:, window(to)], fields.at[me], (field_send, field_recv), k, "member", to))
        pick_copies.append(send(picks.at[to], met.at[me], (pick_send, pick_recv), k, "member", to))
    for copy in slot_copies:
        copy.start()
    slots_met[mine, :] = slot_ref[...]
    fill(table, own_ref, side_ref, tile_obs, 0, tile_obs)
    for copy in slot_copies:
        copy.wait()
    to_smem = pltpu.make_async_copy(slots_met, slots_smem, local.at[1])
    to_smem.start()
    to_smem.wait()
    for copy in side_copies:
        copy.wait()
    for c in range(CHUNKS):
        halo_copies[2 * c].wait()
        fill(table, before, sbefore, 0, c * piece, piece)
        halo_copies[2 * c + 1].wait()
        if c == 0:
            for copy in field_copies:
                copy.start()
        fill(table, after, safter, 2 * tile_obs, c * piece, piece)

    def pick_for(to, own):
        @pl.loop(0, lines)
        def _(r):
            for u in range(128):
                i = slots_smem[to * lines + r, u]
                picked_rows[u:u + 1, :] = table[pl.ds(i, 1), :]
            t = picked_rows[...].T
            block = r // per
            at = pl.ds(pl.multiple_of((r % per) * 128, 128), 128)
            if own:
                met[to, block, :, at] = t[:share].astype(BF16)
                side_met[block, :, at] = t[share:share + 8]
            else:
                picks[to, block, :, at] = t[:share].astype(BF16)

    @pl.loop(1, devices)
    def _(k):
        to = lax.rem(me + k, devices)
        pick_for(to, False)
        send(picks.at[to], met.at[me], (pick_send, pick_recv), k, "member", to).start()

    pick_for(me, True)
    for copy in pick_copies:
        copy.wait()
    copies = []
    for b in range(blocks):
        x = met[:, b].reshape(members, slots).astype(F32)
        zs, halves, pulls = roots(
            [x], [side_met[b, 0:1]], [side_met[b, 1:2]], [bin_ref[b:b + 1]], [count_ref[b]])
        w4 = spread_levels(weights_t(zs[0], halves[0], pulls[0]), levels)
        if b == 0:
            keep.wait()
            for copy in field_copies:
                copy.wait()
        f = fields[:, :, b * cut:(b + 1) * cut].reshape(rows, cut)
        made[b] = analyse(f, w4, levels).reshape(parts, rows // parts, cut)
        window = pl.ds(pl.multiple_of(me * cols + b * cut, 128), cut)
        for k in range(1, parts):
            to = lax.rem(me + k, parts)
            copy = send(made.at[b, to], out_ref.at[:, window], (out_send.at[b], out_recv.at[b]), k, "member", to)
            copy.start()
            copies.append(copy)
        out_ref[:, window] = made[b, me]
    for copy in copies:
        copy.wait()


def per_device(background, obs_ens, observed, variance, obs_slot, obs_count, loc_bin):
    devices = lax.axis_size("member")
    space = lax.axis_size("space")
    share, levels, columns = background.shape
    blocks, width = obs_slot.shape[1:]
    rows, cols = share * levels, columns // devices
    own = obs_ens.astype(BF16)
    side = jnp.concatenate([observed.reshape(-1, 128), variance.reshape(-1, 128)], axis=0)
    slots = obs_slot.reshape(-1, 128)
    flat = background.reshape(rows, columns)
    hbm = pl.BlockSpec(memory_space=pl.ANY)
    vmem = pl.BlockSpec(memory_space=pltpu.VMEM)
    dma = lambda *n: pltpu.SemaphoreType.DMA(n)
    like = jax.ShapeDtypeStruct
    out = pl.pallas_call(
        functools.partial(main_kernel, devices, space, levels),
        out_shape=like((rows, columns), BF16),
        in_specs=[pl.BlockSpec(memory_space=pltpu.SMEM)] + [vmem] * 4 + [hbm],
        out_specs=vmem,
        scratch_shapes=[
            pltpu.VMEM((3 * own.shape[1], 128), F32), pltpu.VMEM((128, 128), F32),
            pltpu.VMEM(own.shape, BF16), pltpu.VMEM(own.shape, BF16),
            pltpu.VMEM(side.shape, F32), pltpu.VMEM(side.shape, F32),
            pltpu.VMEM((devices * slots.shape[0], 128), jnp.int32), pltpu.SMEM((devices * slots.shape[0], 128), jnp.int32),
            pltpu.VMEM((devices, rows, cols), BF16),
            pltpu.VMEM((devices, blocks, share, width), BF16), pltpu.VMEM((devices, blocks, share, width), BF16),
            pltpu.VMEM((blocks, 8, width), F32), pltpu.VMEM((blocks, devices, rows, cols // blocks), BF16),
            dma(2), dma(2 + 2 * CHUNKS), dma(2 + 2 * CHUNKS)] + [dma(devices)] * 6 + [dma(blocks, devices)] * 2,
        compiler_params=pltpu.CompilerParams(collective_id=0, has_side_effects=True, vmem_limit_bytes=50 * 2**20),
        name="analysis",
    )(obs_count[0], own, side, slots, loc_bin[0], flat)
    return out.reshape(share, levels, columns)


def solution(mesh):
    in_specs = (
        P("member", None, "space"), P("member", "space"), P("space"), P("space"),
        P("space", "member", None), P("space", "member"), P("space", "member", None),
    )
    return jax.shard_map(per_device, mesh=mesh, in_specs=in_specs,
                         out_specs=P("member", None, "space"), check_vma=False)
```
